128 devices in a mesh: region: 8 (over z, core), sub: 16 (over y, x).
Axes of the slice: x: 4, y: 4, z: 4, core: 2. Of those that a mesh axis runs over, the one named last changes fastest.
Arguments:
- features: bfloat16 [96, 1048576], P(None, ('region', 'sub')), may hold values from -60 to 60
- neighbors: int32 [27, 1048576], P(None, ('region', 'sub')), may hold values from 0 to 24576, as said below
- send_rows: int32 [128, 16384], P(('region', 'sub')), may hold values from 0 to 8191, as said below
- active_rows: int32 [128], replicated, may hold values from 2048 to 8192, as said below
- weight_one: bfloat16 [27, 96, 96], replicated, may hold values from -0.125 to 0.125
- weight_two: bfloat16 [27, 96, 96], replicated, may hold values from -0.125 to 0.125
- norm_gain: float32 [2, 96], replicated, may hold values from 0.5 to 2
- norm_shift: float32 [2, 96], replicated, may hold values from -1 to 1
Outputs:
- refined: bfloat16 [96, 1048576], P(None, ('region', 'sub'))
The draws below stay inside these ranges and needn't reach their ends.
Inputs may be any that keep to these rules, and one draw needn't show every extreme that they name: `active_rows`: each entry is a multiple of 128; the busiest device has all 8192 slots occupied; occupied slots come first. `send_rows`: row s lists in slots r * 128 to r * 128 + 127 the local columns of device s, below active_rows[s], whose features device r needs; any device r other than s may receive; the slots that carry voxels come first in each group of 128; a slot that carries nothing holds 0; in every draw some device receives all 128 slots from every other device. `neighbors`: an entry is a local column below the device's active count, an arrived column 8192 + p * 128 + c whose slot carries a voxel, or 24576 for a missing voxel; the middle offset of an active column names the column itself; inactive columns name no voxel; every slot that carries a voxel is named somewhere.
All inputs are finite; a program needn't handle non-finite values.
Results may differ from the reference program's by a relative error of at most 0.0052.
Values may be sent and summed in bfloat16 or wider, within the bound.
No kernel may reach another device: no remote copies, remote signals or barrier semaphores. Data moves between devices by JAX's collectives and lax.ppermute only.
A program may use at most 128 MiB of HBM per device.

```python
import math
import jax
import jax.numpy as jnp
from jax import lax

C = 96
K3 = 27
BLOCK = 128
V_DEV = 8192
CAP = 128
DEVICES = 128


def active_counts(key):
    streams = jax.random.split(jax.random.fold_in(key, 7), 8)
    blocks = V_DEV // BLOCK
    lowest = max(1, blocks // 4)
    breadth = blocks - lowest
    draws_blk = jax.random.randint(streams[0], (DEVICES,), 0, breadth + 1)
    count_blk = lowest + draws_blk * draws_blk * draws_blk // max(breadth, 1) ** 2
    order = jax.random.permutation(streams[1], DEVICES)
    count_blk = count_blk.at[order[0]].set(blocks).at[order[1]].set(lowest)
    active = (count_blk * BLOCK).astype(jnp.int32)
    return (active, streams, order)


def layout(key):
    active, streams, order = active_counts(key)
    dev_ids = jnp.arange(DEVICES, dtype=jnp.int32)
    others = dev_ids[:, None] != dev_ids[None, :]
    sends = jax.random.randint(streams[2], (DEVICES, DEVICES), 0, CAP + 1)
    sends = jnp.where(others, sends, 0)
    sends = sends.at[:, order[2]].set(jnp.where(others[:, order[2]], CAP, 0))
    slot_ids = jnp.arange(CAP, dtype=jnp.int32)
    listed = jax.random.randint(streams[3], (DEVICES, DEVICES, CAP), 0, active[:, None, None])
    listed = jnp.where(slot_ids[None, None, :] < sends[:, :, None], listed, 0)
    send_table = listed.reshape(DEVICES, DEVICES * CAP).astype(jnp.int32)
    missing = V_DEV + DEVICES * CAP

    def device_map(dev_key, active_count, recv_counts):
        pieces = jax.random.split(dev_key, 4)
        columns = jnp.arange(V_DEV, dtype=jnp.int32)
        living = columns < active_count
        sort_kind = jax.random.randint(pieces[0], (K3, V_DEV), 0, 8)
        local_pick = jax.random.randint(pieces[1], (K3, V_DEV), 0, active_count)
        slots = jnp.arange(DEVICES * CAP, dtype=jnp.int32)
        carrying = slots % CAP < recv_counts[slots // CAP]
        slot_order = jnp.argsort(jnp.where(carrying, 0, 1) * (DEVICES * CAP) + slots, stable=True).astype(jnp.int32)
        held = jnp.sum(carrying.astype(jnp.int32))
        halo_pick = jax.random.randint(pieces[2], (K3, V_DEV), 0, jnp.maximum(held, 1))
        halo_ref = V_DEV + slot_order[halo_pick]
        kernel_map = jnp.where(sort_kind <= 1, missing, jnp.where(sort_kind == 7, jnp.where(held > 0, halo_ref, missing), local_pick))
        kernel_map = kernel_map.at[K3 // 2].set(columns)
        kernel_map = jnp.where(living[None, :], kernel_map, missing)
        flat_map = kernel_map.reshape(-1)
        usable = (living[None, :] & (jnp.arange(K3)[:, None] != K3 // 2)).reshape(-1)
        shuffle = jax.random.permutation(pieces[3], K3 * V_DEV)
        pos_order = jnp.argsort(jnp.where(usable, 0, 1) * (K3 * V_DEV) + shuffle, stable=True)
        targets = pos_order[:DEVICES * CAP]
        rank_ids = jnp.arange(DEVICES * CAP, dtype=jnp.int32)
        flat_map = flat_map.at[targets].set(jnp.where(rank_ids < held, V_DEV + slot_order, flat_map[targets]))
        return flat_map.reshape(K3, V_DEV).astype(jnp.int32)
    dev_keys = jax.random.split(streams[4], DEVICES)
    maps = jax.vmap(device_map)(dev_keys, active, sends.T)
    neighbor_table = jnp.transpose(maps, (1, 0, 2)).reshape(K3, DEVICES * V_DEV)
    return (active, send_table, neighbor_table)


def draw_active_rows(key, part):
    return layout(key)[0]


def draw_send_rows(key, part):
    return layout(key)[1]


def draw_neighbors(key, part):
    return layout(key)[2]


def draw_features(key, part):
    active = active_counts(key)[0]
    streams = jax.random.split(jax.random.fold_in(key, 11), 3)
    total_rows = DEVICES * V_DEV
    row_ids = jnp.arange(total_rows, dtype=jnp.int32)
    position = row_ids.astype(jnp.float32) / max(total_rows - 1, 1)
    owner = row_ids // V_DEV
    column = (row_ids % V_DEV).astype(jnp.float32)
    span = jnp.maximum(active[owner] - 1, 1).astype(jnp.float32)
    inner = jnp.clip(column / span, 0.0, 1.0)
    row_draw = jax.random.uniform(streams[0], (total_rows,), jnp.float32)
    col_draw = jax.random.uniform(streams[1], (C, 1), jnp.float32)
    row_scale = jnp.power(10.0, 0.35 * position + 0.45 * inner + 0.2 * row_draw)
    basis = jnp.clip(jax.random.normal(streams[2], (C, total_rows), jnp.float32), -6.0, 6.0)
    values = 0.1 * basis * row_scale[None, :] * jnp.power(10.0, col_draw)
    return values.astype(jnp.bfloat16)


def normal_values(own_key, dims, width, reach, kind=jnp.bfloat16):
    return jnp.clip(width * jax.random.normal(own_key, dims, jnp.float32), -reach, reach).astype(kind)


def setup_inputs(seed: int = 0) -> dict:
    key_of = jax.random.split(jax.random.key(seed), 9)
    features = draw_features(jax.random.fold_in(key_of[8], 71), 0)
    neighbors = draw_neighbors(jax.random.fold_in(key_of[8], 71), 0)
    send_rows = draw_send_rows(jax.random.fold_in(key_of[8], 71), 0)
    active_rows = draw_active_rows(jax.random.fold_in(key_of[8], 71), 0)
    weight_one = normal_values(key_of[4], (K3, C, C), (K3 * C) ** -0.5, 0.125)
    weight_two = normal_values(key_of[5], (K3, C, C), (K3 * C) ** -0.5, 0.125)
    norm_gain = jnp.clip(jnp.exp(jax.random.uniform(key_of[6], (2, C), jnp.float32, math.log(0.5), math.log(2.0))), 0.5, 2.0)
    norm_shift = jnp.clip(jax.random.uniform(key_of[7], (2, C), jnp.float32, -1.0, 1.0), -1.0, 1.0)
    return dict(features=features, neighbors=neighbors, send_rows=send_rows, active_rows=active_rows, weight_one=weight_one, weight_two=weight_two, norm_gain=norm_gain, norm_shift=norm_shift)


NORM_EPS = 1e-05

def gather_columns(extended, kernel_map, weight):
    gathered = jnp.take(extended, kernel_map, axis=1, mode='fill', fill_value=0)
    return jnp.einsum('ikb,kio->ob', gathered.astype(jnp.float32), weight.astype(jnp.float32))

def one_layer(hidden, neighbors, send_rows, active_rows, weight, gain, shift):

    def device_conv(device):
        own = lax.dynamic_slice_in_dim(hidden, device * V_DEV, V_DEV, 1)
        listed = lax.dynamic_slice_in_dim(send_rows, device * CAP, CAP, 1).astype(jnp.int32)
        sources = (jnp.arange(DEVICES, dtype=jnp.int32)[:, None] * V_DEV + listed).reshape(-1)
        arrived = jnp.take(hidden, sources, axis=1)
        extended = jnp.concatenate([own, arrived], axis=1)
        kernel_map = lax.dynamic_slice_in_dim(neighbors, device * V_DEV, V_DEV, 1)
        return gather_columns(extended, kernel_map, weight)
    conved = lax.map(device_conv, jnp.arange(DEVICES, dtype=jnp.int32))
    active = jnp.arange(V_DEV, dtype=jnp.int32)[None, None, :] < active_rows[:, None, None]
    population = jnp.sum(active_rows).astype(jnp.float32)
    average = lax.optimization_barrier(jnp.sum(jnp.where(active, conved, 0.0), axis=(0, 2))) / population
    offset = jnp.where(active, conved - average[None, :, None], 0.0)
    spread = lax.optimization_barrier(jnp.sum(offset * offset, axis=(0, 2))) / population
    factor = gain * lax.rsqrt(spread + NORM_EPS)
    normed = (conved - average[None, :, None]) * factor[None, :, None] + shift[None, :, None]
    normed = jnp.where(active, jnp.maximum(normed, 0.0), 0.0).astype(jnp.bfloat16)
    return jnp.transpose(normed, (1, 0, 2)).reshape(normed.shape[1], -1)

def reference(features, neighbors, send_rows, active_rows, weight_one, weight_two, norm_gain, norm_shift):
    level_one = one_layer(features, neighbors, send_rows, active_rows, weight_one, norm_gain[0], norm_shift[0])
    return one_layer(level_one, neighbors, send_rows, active_rows, weight_two, norm_gain[1], norm_shift[1])
```

```python
import functools

import jax
import jax.numpy as jnp
from jax import lax
from jax.experimental import pallas as pl
from jax.experimental.pallas import tpu as pltpu
from jax.sharding import PartitionSpec as P

AXES = ("region", "sub")
C = 96
K3 = 27
MID = K3 // 2
PAIRS = MID
BLOCK = 128
LANES = 128
V_DEV = 8192
CAP = 128
DEVICES = 128
ARRIVED = DEVICES * CAP
MISSING = V_DEV + ARRIVED
NORM_EPS = 1e-05
VMEM_LIMIT = 60 << 20
TAIL = CAP - C
LOW = 0x7FFF

F32 = jnp.float32
BF16 = jnp.bfloat16
IN_VMEM = pl.BlockSpec(memory_space=pltpu.VMEM)
IN_SMEM = pl.BlockSpec(memory_space=pltpu.SMEM)
IN_ANY = pl.BlockSpec(memory_space=pl.ANY)


def moments(stats, counts):
    means, squares = stats[:, 0, :], stats[:, 1, :]
    population = jnp.sum(counts, axis=0, keepdims=True)
    average = jnp.sum(means * counts, axis=0, keepdims=True) / population
    apart = means - average
    spread = jnp.sum(squares + counts * apart * apart, axis=0, keepdims=True) / population
    return average, spread


def send_rows_packed(picks, table, stage, out):
    lane = lax.broadcasted_iota(jnp.int32, (TAIL, LANES), 1)

    def pack(d, slot):
        last = stage[slot, C:CAP, :]
        for j in range(C // TAIL):
            rows = stage[slot, j * TAIL : (j + 1) * TAIL, :]
            moved = pltpu.roll(last, C - j * TAIL, 1) if j < C // TAIL else last
            out[d, j * TAIL : (j + 1) * TAIL, :] = jnp.where(lane < C, rows, moved).astype(BF16)

    def collect(d, slot):
        for c in range(CAP // 2):
            both = picks[d, c]
            stage[slot, c : c + 1, :] = table[pl.ds(both & LOW, 1), :]
            stage[slot, c + CAP // 2 : c + CAP // 2 + 1, :] = table[pl.ds(both >> 16, 1), :]

    collect(0, 0)

    def advance(d, carry):
        pack(d - 1, (d - 1) % 2)
        collect(d, d % 2)
        return carry

    lax.fori_loop(1, DEVICES, advance, 0)
    pack(DEVICES - 1, (DEVICES - 1) % 2)


def first_send_kernel(picks, own, out, table, stage):
    def fill(b, carry):
        rows = pl.ds(pl.multiple_of(b * BLOCK, BLOCK), BLOCK)
        table[rows, 0:C] = own[rows, :].astype(F32)
        return carry

    table[:, C:LANES] = jnp.zeros((V_DEV, LANES - C), F32)
    lax.fori_loop(0, V_DEV // BLOCK, fill, 0)
    send_rows_packed(picks, table, stage, out)


def next_send_kernel(picks, live, conved, stats, counts, gain, shift, out, own, table, stage):
    average, spread = moments(stats, counts[...])
    factor = gain[...] * lax.rsqrt(spread + NORM_EPS)
    offset = shift[...]
    blocks = live[0] // BLOCK

    def fill(b, carry):
        rows = pl.ds(pl.multiple_of(b * BLOCK, BLOCK), BLOCK)
        normed = (conved[rows, :] - average) * factor + offset
        hidden = jnp.maximum(normed, 0.0).astype(BF16)
        own[rows, :] = hidden
        table[rows, :] = hidden.astype(F32)
        return carry

    def clear(b, carry):
        rows = pl.ds(pl.multiple_of(b * BLOCK, BLOCK), BLOCK)
        own[rows, :] = jnp.zeros((BLOCK, LANES), BF16)
        return carry

    lax.fori_loop(0, blocks, fill, 0)
    lax.fori_loop(blocks, V_DEV // BLOCK, clear, 0)
    send_rows_packed(picks, table, stage, out)


def conv_kernel(live, index_hbm, own, arrived, weight, middle, out, stats, table, stage, index, sem):
    load = pltpu.make_async_copy(index_hbm, index, sem)
    load.start()
    blocks = live[0] // BLOCK
    width = own.shape[1]
    lane = lax.broadcasted_iota(jnp.int32, (TAIL, LANES), 1)

    def fill_own(b, carry):
        rows = pl.ds(pl.multiple_of(b * BLOCK, BLOCK), BLOCK)
        table[rows, 0:width] = own[rows, :].astype(F32)
        if width < LANES:
            table[rows, width:LANES] = jnp.zeros((BLOCK, LANES - width), F32)
        return carry

    def fill_arrived(p, carry):
        base = pl.multiple_of(V_DEV + p * CAP, CAP)
        rows = arrived[p].astype(F32)
        table[pl.ds(base, C), :] = rows
        tail = None
        for j in range(C // TAIL):
            moved = pltpu.roll(rows[j * TAIL : (j + 1) * TAIL], TAIL * (j + 1), 1)
            tail = moved if tail is None else jnp.where(lane < j * TAIL, tail, moved)
        table[pl.ds(base + C, TAIL), :] = tail
        return carry

    lax.fori_loop(0, V_DEV // BLOCK, fill_own, 0)
    lax.fori_loop(0, DEVICES, fill_arrived, 0)
    table[MISSING : MISSING + 8, :] = jnp.zeros((8, LANES), F32)
    load.wait()

    def multiply(slot, p):
        return jnp.dot(stage[slot, p].astype(BF16), weight[p], preferred_element_type=F32)

    def collect(block, slot, p):
        for c in range(BLOCK):
            both = index[block * PAIRS + p, c]
            stage[slot, p, c : c + 1, 0:LANES] = table[pl.ds(both & LOW, 1), :]
            stage[slot, p, c : c + 1, LANES : 2 * LANES] = table[pl.ds(both >> 16, 1), :]

    def center(block):
        rows = pl.ds(pl.multiple_of(block * BLOCK, BLOCK), BLOCK)
        return jnp.dot(table[rows, :].astype(BF16), middle[...], preferred_element_type=F32)

    def finish(block, total, sums):
        out[pl.ds(pl.multiple_of(block * BLOCK, BLOCK), BLOCK), :] = total
        return sums + jnp.sum(total.reshape(BLOCK // 8, 8, LANES), axis=0)

    def first(p, carry):
        collect(0, 0, p)
        return carry

    lax.fori_loop(0, PAIRS, first, 0)

    def advance(block, sums):
        now = block % 2

        def pair(p, total):
            total = total + multiply(1 - now, p)
            collect(block, now, p)
            return total

        total = lax.fori_loop(0, PAIRS, pair, center(block - 1))
        return finish(block - 1, total, sums)

    sums = lax.fori_loop(1, blocks, advance, jnp.zeros((8, LANES), F32))
    last = blocks - 1
    total = center(last)
    for p in range(PAIRS):
        total = total + multiply(last % 2, p)
    sums = finish(last, total, sums)

    count = (blocks * BLOCK).astype(F32)
    average = jnp.sum(sums, axis=0, keepdims=True) / count

    def deviate(block, squares):
        rows = pl.ds(pl.multiple_of(block * BLOCK, BLOCK), BLOCK)
        apart = out[rows, :] - average
        return squares + jnp.sum((apart * apart).reshape(BLOCK // 8, 8, LANES), axis=0)

    squares = lax.fori_loop(0, blocks, deviate, jnp.zeros((8, LANES), F32))
    stats[0:1, :] = average
    stats[1:2, :] = jnp.sum(squares, axis=0, keepdims=True)


def last_kernel(live, conved, stats, counts, gain, shift, out):
    step = pl.program_id(0)
    average, spread = moments(stats, counts[...])
    factor = gain[...] * lax.rsqrt(spread + NORM_EPS)
    size = conved.shape[0]
    row = lax.broadcasted_iota(jnp.int32, (size, LANES), 0) + step * size
    normed = jnp.maximum((conved[...] - average) * factor + shift[...], 0.0)
    normed = jnp.where(row < live[0], normed, 0.0)
    out[...] = jnp.transpose(normed)[0:C, :].astype(BF16)


def params():
    return pltpu.CompilerParams(vmem_limit_bytes=VMEM_LIMIT)


def first_send(picks, own):
    return pl.pallas_call(
        first_send_kernel,
        in_specs=[IN_SMEM, IN_VMEM],
        out_specs=IN_VMEM,
        out_shape=jax.ShapeDtypeStruct((DEVICES, C, LANES), BF16),
        scratch_shapes=[pltpu.VMEM((V_DEV, LANES), F32), pltpu.VMEM((2, CAP, LANES), F32)],
        compiler_params=params(),
        name="first_send",
    )(picks, own)


def next_send(picks, live, conved, stats, counts, gain, shift):
    return pl.pallas_call(
        next_send_kernel,
        in_specs=[IN_SMEM, IN_SMEM] + [IN_VMEM] * 5,
        out_specs=[IN_VMEM, IN_VMEM],
        out_shape=[
            jax.ShapeDtypeStruct((DEVICES, C, LANES), BF16),
            jax.ShapeDtypeStruct((V_DEV, LANES), BF16),
        ],
        scratch_shapes=[pltpu.VMEM((V_DEV, LANES), F32), pltpu.VMEM((2, CAP, LANES), F32)],
        compiler_params=params(),
        name="next_send",
    )(picks, live, conved, stats, counts, gain, shift)


def convolve(live, index, own, arrived, weight, middle):
    return pl.pallas_call(
        conv_kernel,
        in_specs=[IN_SMEM, IN_ANY] + [IN_VMEM] * 4,
        out_specs=[IN_VMEM, IN_VMEM],
        out_shape=[
            jax.ShapeDtypeStruct((V_DEV, LANES), F32),
            jax.ShapeDtypeStruct((2, LANES), F32),
        ],
        scratch_shapes=[
            pltpu.VMEM((MISSING + 8, LANES), F32),
            pltpu.VMEM((2, PAIRS, BLOCK, 2 * LANES), F32),
            pltpu.SMEM((V_DEV // BLOCK * PAIRS, BLOCK), jnp.int32),
            pltpu.SemaphoreType.DMA,
        ],
        compiler_params=params(),
        name="sparse_conv",
    )(live, index, own, arrived, weight, middle)


def last_norm(live, conved, stats, counts, gain, shift):
    size = 1024
    whole = lambda *dims: pl.BlockSpec(dims, lambda i: (0,) * len(dims))
    return pl.pallas_call(
        last_kernel,
        grid=(V_DEV // size,),
        in_specs=[
            IN_SMEM,
            pl.BlockSpec((size, LANES), lambda i: (i, 0)),
            whole(DEVICES, 2, LANES),
            whole(DEVICES, LANES),
            whole(1, LANES),
            whole(1, LANES),
        ],
        out_specs=pl.BlockSpec((C, size), lambda i: (0, i)),
        out_shape=jax.ShapeDtypeStruct((C, V_DEV), BF16),
        compiler_params=params(),
        name="last_norm",
    )(live, conved, stats, counts, gain, shift)


def exchange(parcels):
    return lax.all_to_all(parcels, AXES, split_axis=0, concat_axis=0, tiled=True)


def share(stats):
    return exchange(jnp.broadcast_to(stats[None], (DEVICES, 2, LANES)))


def prepare_weight(weight):
    wide = jnp.pad(weight, ((0, 0), (0, LANES - C), (0, LANES - C)))
    return jnp.concatenate([wide[:MID], wide[MID + 1 :]], axis=1), wide[MID]


def body(
    features, neighbors, send_rows, active_rows, weight_one, weight_two, norm_gain, norm_shift
):
    device = lax.axis_index(AXES)
    live = lax.dynamic_slice_in_dim(active_rows, device, 1)
    counts = jnp.broadcast_to(active_rows.astype(F32)[:, None], (DEVICES, LANES))
    gain = jnp.pad(norm_gain, ((0, 0), (0, LANES - C)))
    shift = jnp.pad(norm_shift, ((0, 0), (0, LANES - C)))
    listed = send_rows.reshape(DEVICES, CAP)
    picks = listed[:, : CAP // 2] | (listed[:, CAP // 2 :] << 16)
    index = neighbors[:MID] | (neighbors[MID + 1 :] << 16)
    index = index.reshape(PAIRS, V_DEV // BLOCK, BLOCK).transpose(1, 0, 2).reshape(-1, BLOCK)

    own = jnp.transpose(features)
    arrived = exchange(first_send(picks, own))
    conved, stats = convolve(live, index, own, arrived, *prepare_weight(weight_one))
    stats = share(stats)
    parcels, own = next_send(picks, live, conved, stats, counts, gain[0:1], shift[0:1])
    arrived = exchange(parcels)
    conved, stats = convolve(live, index, own, arrived, *prepare_weight(weight_two))
    stats = share(stats)
    return last_norm(live, conved, stats, counts, gain[1:2], shift[1:2])


def solution(mesh):
    placed = (
        P(None, AXES),
        P(None, AXES),
        P(AXES, None),
        P(),
        P(),
        P(),
        P(),
        P(),
    )
    return jax.shard_map(
        body, mesh=mesh, in_specs=placed, out_specs=P(None, AXES), check_vma=False
    )
```

```python
import functools

import jax
import jax.numpy as jnp
from jax import lax
from jax.experimental import pallas as pl
from jax.experimental.pallas import tpu as pltpu
from jax.sharding import PartitionSpec as P

AXES = ("region", "sub")
C = 96
K3 = 27
MID = K3 // 2
PAIRS = MID
BLOCK = 128
LANES = 128
V_DEV = 8192
CAP = 128
GROUP = 8
SLOTS = 4
DEVICES = 128
ARRIVED = DEVICES * CAP
MISSING = V_DEV + ARRIVED
NORM_EPS = 1e-05
VMEM_LIMIT = 60 << 20
TAIL = CAP - C

F32 = jnp.float32
BF16 = jnp.bfloat16
IN_VMEM = pl.BlockSpec(memory_space=pltpu.VMEM)
IN_SMEM = pl.BlockSpec(memory_space=pltpu.SMEM)
IN_ANY = pl.BlockSpec(memory_space=pl.ANY)


def moments(stats, counts):
    means, squares = stats[:, 0, :], stats[:, 1, :]
    population = jnp.sum(counts, axis=0, keepdims=True)
    average = jnp.sum(means * counts, axis=0, keepdims=True) / population
    apart = means - average
    spread = jnp.sum(squares + counts * apart * apart, axis=0, keepdims=True) / population
    return average, spread


def send_rows_packed(picks, table, stage, out, index, sems):
    lane = lax.broadcasted_iota(jnp.int32, (TAIL, LANES), 1)
    groups = DEVICES // GROUP

    def fetch(g, slot):
        return pltpu.make_async_copy(picks.at[g], index.at[slot], sems.at[slot])

    def pack(d, j):
        last = stage[j, C:CAP, :]
        for t in range(C // TAIL):
            rows = stage[j, t * TAIL : (t + 1) * TAIL, :]
            moved = pltpu.roll(last, C - t * TAIL, 1)
            out[d, t * TAIL : (t + 1) * TAIL, :] = jnp.where(lane < C, rows, moved).astype(BF16)

    def group(g, slot):
        for j in range(GROUP):
            pack(jnp.maximum(g - 1, 0) * GROUP + j, j)
            for c in range(CAP):
                stage[j, c : c + 1, :] = table[pl.ds(index[slot, j, c], 1), :]

    def advance(r, carry):
        for slot in range(SLOTS):
            g = r * SLOTS + slot
            fetch(g, slot).wait()
            group(g, slot)

            @pl.when(g + SLOTS < groups)
            def _():
                fetch(g + SLOTS, slot).start()

        return carry

    lax.fori_loop(0, groups // SLOTS, advance, 0)
    for j in range(GROUP):
        pack(DEVICES - GROUP + j, j)


def start_picks(picks, index, sems):
    for slot in range(SLOTS):
        pltpu.make_async_copy(picks.at[slot], index.at[slot], sems.at[slot]).start()


def first_send_kernel(picks, own, out, table, stage, index, sems):
    start_picks(picks, index, sems)

    def fill(b, carry):
        rows = pl.ds(pl.multiple_of(b * BLOCK, BLOCK), BLOCK)
        table[rows, :] = own[rows, :].astype(F32)
        return carry

    lax.fori_loop(0, V_DEV // BLOCK, fill, 0)
    send_rows_packed(picks, table, stage, out, index, sems)


def next_send_kernel(
    picks, live, conved, stats, counts, gain, shift, out, own, table, stage, index, sems
):
    start_picks(picks, index, sems)
    average, spread = moments(stats, counts[...])
    factor = gain[...] * lax.rsqrt(spread + NORM_EPS)
    offset = shift[...]
    blocks = live[0] // BLOCK

    def fill(b, carry):
        rows = pl.ds(pl.multiple_of(b * BLOCK, BLOCK), BLOCK)
        normed = (conved[rows, :] - average) * factor + offset
        hidden = jnp.maximum(normed, 0.0).astype(BF16)
        own[rows, :] = hidden
        table[rows, :] = hidden.astype(F32)
        return carry

    def clear(b, carry):
        rows = pl.ds(pl.multiple_of(b * BLOCK, BLOCK), BLOCK)
        own[rows, :] = jnp.zeros((BLOCK, LANES), BF16)
        return carry

    lax.fori_loop(0, blocks, fill, 0)
    lax.fori_loop(blocks, V_DEV // BLOCK, clear, 0)
    send_rows_packed(picks, table, stage, out, index, sems)


def conv_kernel(live, maps, own, arrived, weight, middle, out, stats, table, stage, sums, index, sems):
    def fetch(block, slot):
        columns = pl.ds(pl.multiple_of(block * BLOCK, BLOCK), BLOCK)
        return pltpu.make_async_copy(maps.at[:, columns], index.at[slot], sems.at[slot])

    fetch(0, 0).start()
    blocks = live[0] // BLOCK
    lane = lax.broadcasted_iota(jnp.int32, (TAIL, LANES), 1)

    def fill_own(b, carry):
        rows = pl.ds(pl.multiple_of(b * BLOCK, BLOCK), BLOCK)
        table[rows, :] = own[rows, :].astype(F32)
        return carry

    def fill_arrived(p, carry):
        base = pl.multiple_of(V_DEV + p * CAP, CAP)
        rows = arrived[p].astype(F32)
        table[pl.ds(base, C), :] = rows
        tail = None
        for j in range(C // TAIL):
            moved = pltpu.roll(rows[j * TAIL : (j + 1) * TAIL], TAIL * (j + 1), 1)
            tail = moved if tail is None else jnp.where(lane < j * TAIL, tail, moved)
        table[pl.ds(base + C, TAIL), :] = tail
        return carry

    lax.fori_loop(0, V_DEV // BLOCK, fill_own, 0)
    lax.fori_loop(0, DEVICES, fill_arrived, 0)
    table[MISSING : MISSING + 8, :] = jnp.zeros((8, LANES), F32)

    def multiply(slot, p):
        return jnp.dot(stage[slot, p].astype(BF16), weight[p], preferred_element_type=F32)

    def collect(slot, p):
        for c in range(BLOCK):
            low, high = index[slot, p, c], index[slot, MID + 1 + p, c]
            stage[slot, p, c : c + 1, 0:LANES] = table[pl.ds(low, 1), :]
            stage[slot, p, c : c + 1, LANES : 2 * LANES] = table[pl.ds(high, 1), :]

    def center(block):
        rows = pl.ds(pl.multiple_of(block * BLOCK, BLOCK), BLOCK)
        return jnp.dot(table[rows, :].astype(BF16), middle[...], preferred_element_type=F32)

    def finish(block, total):
        out[pl.ds(pl.multiple_of(block * BLOCK, BLOCK), BLOCK), :] = total
        return jnp.sum(total.reshape(BLOCK // 8, 8, LANES), axis=0)

    def step(block, slot):
        fetch(block, slot).wait()

        @pl.when(block + 1 < blocks)
        def _():
            fetch(block + 1, 1 - slot).start()

        before = jnp.maximum(block - 1, 0)
        total = center(before)
        for p in range(PAIRS):
            total = total + multiply(1 - slot, p)
            collect(slot, p)
        part = finish(before, total)
        sums[...] = jnp.where(block > 0, sums[...] + part, 0.0)

    def advance(block, carry):
        for slot in range(2):
            pl.when(block % 2 == slot)(functools.partial(step, block, slot))
        return carry

    sums[...] = jnp.zeros((8, LANES), F32)
    lax.fori_loop(0, blocks, advance, 0)
    last = blocks - 1
    total = center(last)
    for p in range(PAIRS):
        total = total + multiply(last % 2, p)
    sums[...] += finish(last, total)

    count = (blocks * BLOCK).astype(F32)
    average = jnp.sum(sums[...], axis=0, keepdims=True) / count

    def deviate(block, squares):
        rows = pl.ds(pl.multiple_of(block * BLOCK, BLOCK), BLOCK)
        apart = out[rows, :] - average
        return squares + jnp.sum((apart * apart).reshape(BLOCK // 8, 8, LANES), axis=0)

    squares = lax.fori_loop(0, blocks, deviate, jnp.zeros((8, LANES), F32))
    stats[0:1, :] = average
    stats[1:2, :] = jnp.sum(squares, axis=0, keepdims=True)


def last_kernel(live, conved, stats, counts, gain, shift, out):
    step = pl.program_id(0)
    average, spread = moments(stats, counts[...])
    factor = gain[...] * lax.rsqrt(spread + NORM_EPS)
    size = conved.shape[0]
    row = lax.broadcasted_iota(jnp.int32, (size, LANES), 0) + step * size
    normed = jnp.maximum((conved[...] - average) * factor + shift[...], 0.0)
    normed = jnp.where(row < live[0], normed, 0.0)
    out[...] = jnp.transpose(normed)[0:C, :].astype(BF16)


def params():
    return pltpu.CompilerParams(vmem_limit_bytes=VMEM_LIMIT)


def send_scratch():
    return [
        pltpu.VMEM((V_DEV, LANES), F32),
        pltpu.VMEM((GROUP, CAP, LANES), F32),
        pltpu.SMEM((SLOTS, GROUP, CAP), jnp.int32),
        pltpu.SemaphoreType.DMA((SLOTS,)),
    ]


def first_send(picks, own):
    return pl.pallas_call(
        first_send_kernel,
        in_specs=[IN_ANY, IN_VMEM],
        out_specs=IN_VMEM,
        out_shape=jax.ShapeDtypeStruct((DEVICES, C, LANES), BF16),
        scratch_shapes=send_scratch(),
        compiler_params=params(),
        name="first_send",
    )(picks, own)


def next_send(picks, live, conved, stats, counts, gain, shift):
    return pl.pallas_call(
        next_send_kernel,
        in_specs=[IN_ANY, IN_SMEM] + [IN_VMEM] * 5,
        out_specs=[IN_VMEM, IN_VMEM],
        out_shape=[
            jax.ShapeDtypeStruct((DEVICES, C, LANES), BF16),
            jax.ShapeDtypeStruct((V_DEV, LANES), BF16),
        ],
        scratch_shapes=send_scratch(),
        compiler_params=params(),
        name="next_send",
    )(picks, live, conved, stats, counts, gain, shift)


@jax.jit
def convolve(live, maps, own, arrived, weight, middle):
    return pl.pallas_call(
        conv_kernel,
        in_specs=[IN_SMEM, IN_ANY] + [IN_VMEM] * 4,
        out_specs=[IN_VMEM, IN_VMEM],
        out_shape=[
            jax.ShapeDtypeStruct((V_DEV, LANES), F32),
            jax.ShapeDtypeStruct((2, LANES), F32),
        ],
        scratch_shapes=[
            pltpu.VMEM((MISSING + 8, LANES), F32),
            pltpu.VMEM((2, PAIRS, BLOCK, 2 * LANES), F32),
            pltpu.VMEM((8, LANES), F32),
            pltpu.SMEM((2, K3, BLOCK), jnp.int32),
            pltpu.SemaphoreType.DMA((2,)),
        ],
        compiler_params=params(),
        name="sparse_conv",
    )(live, maps, own, arrived, weight, middle)


def last_norm(live, conved, stats, counts, gain, shift):
    size = 1024
    whole = lambda *dims: pl.BlockSpec(dims, lambda i: (0,) * len(dims))
    return pl.pallas_call(
        last_kernel,
        grid=(V_DEV // size,),
        in_specs=[
            IN_SMEM,
            pl.BlockSpec((size, LANES), lambda i: (i, 0)),
            whole(DEVICES, 2, LANES),
            whole(DEVICES, LANES),
            whole(1, LANES),
            whole(1, LANES),
        ],
        out_specs=pl.BlockSpec((C, size), lambda i: (0, i)),
        out_shape=jax.ShapeDtypeStruct((C, V_DEV), BF16),
        compiler_params=params(),
        name="last_norm",
    )(live, conved, stats, counts, gain, shift)


def exchange(parcels):
    return lax.all_to_all(parcels, AXES, split_axis=0, concat_axis=0, tiled=True)


def share(stats):
    return exchange(jnp.broadcast_to(stats[None], (DEVICES, 2, LANES)))


def prepare_weight(weight):
    wide = jnp.pad(weight, ((0, 0), (0, LANES - C), (0, LANES - C)))
    return jnp.concatenate([wide[:MID], wide[MID + 1 :]], axis=1), wide[MID]


def body(
    features, neighbors, send_rows, active_rows, weight_one, weight_two, norm_gain, norm_shift
):
    device = lax.axis_index(AXES)
    live = lax.dynamic_slice_in_dim(active_rows, device, 1)
    counts = jnp.broadcast_to(active_rows.astype(F32)[:, None], (DEVICES, LANES))
    gain = jnp.pad(norm_gain, ((0, 0), (0, LANES - C)))
    shift = jnp.pad(norm_shift, ((0, 0), (0, LANES - C)))
    picks = send_rows.reshape(DEVICES // GROUP, GROUP, CAP)

    own = jnp.pad(jnp.transpose(features), ((0, 0), (0, LANES - C)))
    arrived = exchange(first_send(picks, own))
    conved, stats = convolve(live, neighbors, own, arrived, *prepare_weight(weight_one))
    stats = share(stats)
    parcels, own = next_send(picks, live, conved, stats, counts, gain[0:1], shift[0:1])
    arrived = exchange(parcels)
    conved, stats = convolve(live, neighbors, own, arrived, *prepare_weight(weight_two))
    stats = share(stats)
    return last_norm(live, conved, stats, counts, gain[1:2], shift[1:2])


def solution(mesh):
    placed = (
        P(None, AXES),
        P(None, AXES),
        P(AXES, None),
        P(),
        P(),
        P(),
        P(),
        P(),
    )
    return jax.shard_map(
        body, mesh=mesh, in_specs=placed, out_specs=P(None, AXES), check_vma=False
    )
```

```python
import functools

import jax
import jax.numpy as jnp
from jax import lax
from jax.experimental import pallas as pl
from jax.experimental.pallas import tpu as pltpu
from jax.sharding import PartitionSpec as P

AXES = ("region", "sub")
C = 96
K3 = 27
MID = K3 // 2
PAIRS = MID
BLOCK = 128
LANES = 128
V_DEV = 8192
CAP = 128
GROUP = 8
SLOTS = 4
DEVICES = 128
ARRIVED = DEVICES * CAP
MISSING = V_DEV + ARRIVED
NORM_EPS = 1e-05
VMEM_LIMIT = 60 << 20
TAIL = CAP - C

F32 = jnp.float32
BF16 = jnp.bfloat16
IN_VMEM = pl.BlockSpec(memory_space=pltpu.VMEM)
IN_SMEM = pl.BlockSpec(memory_space=pltpu.SMEM)
IN_ANY = pl.BlockSpec(memory_space=pl.ANY)


def widen(rows):
    return jnp.concatenate([rows, jnp.zeros((rows.shape[0], LANES - C), rows.dtype)], axis=1)


def moments(stats):
    means, squares = stats[:, 0, :], stats[:, 1, :]
    counts = squares[:, LANES - 1 : LANES]
    population = jnp.sum(counts, axis=0, keepdims=True)
    average = jnp.sum(means * counts, axis=0, keepdims=True) / population
    apart = means - average
    spread = jnp.sum(squares + counts * apart * apart, axis=0, keepdims=True) / population
    return average, spread


def send_rows_packed(picks, table, stage, out, index, sems):
    lane = lax.broadcasted_iota(jnp.int32, (TAIL, LANES), 1)
    groups = DEVICES // GROUP

    def fetch(g, slot):
        return pltpu.make_async_copy(picks.at[g], index.at[slot], sems.at[slot])

    def pack(d, j):
        last = stage[j, C:CAP, :]
        for t in range(C // TAIL):
            rows = stage[j, t * TAIL : (t + 1) * TAIL, :]
            moved = pltpu.roll(last, C - t * TAIL, 1)
            out[d, t * TAIL : (t + 1) * TAIL, :] = jnp.where(lane < C, rows, moved).astype(BF16)

    def group(g, slot):
        for j in range(GROUP):
            pack(jnp.maximum(g - 1, 0) * GROUP + j, j)
            for c in range(CAP):
                stage[j, c : c + 1, :] = table[pl.ds(index[slot, j, c], 1), :]

    def advance(r, carry):
        for slot in range(SLOTS):
            g = r * SLOTS + slot
            fetch(g, slot).wait()
            group(g, slot)

            @pl.when(g + SLOTS < groups)
            def _():
                fetch(g + SLOTS, slot).start()

        return carry

    lax.fori_loop(0, groups // SLOTS, advance, 0)
    for j in range(GROUP):
        pack(DEVICES - GROUP + j, j)


def start_picks(picks, index, sems):
    for slot in range(SLOTS):
        pltpu.make_async_copy(picks.at[slot], index.at[slot], sems.at[slot]).start()


def first_send_kernel(picks, own, out, table, stage, index, sems):
    start_picks(picks, index, sems)

    def fill(b, carry):
        rows = pl.ds(pl.multiple_of(b * BLOCK, BLOCK), BLOCK)
        table[rows, :] = widen(own[rows, :].astype(F32))
        return carry

    lax.fori_loop(0, V_DEV // BLOCK, fill, 0)
    send_rows_packed(picks, table, stage, out, index, sems)


def next_send_kernel(
    picks, live, conved, stats, gain, shift, out, own, table, stage, index, sems
):
    start_picks(picks, index, sems)
    average, spread = moments(stats)
    factor = gain[...] * lax.rsqrt(spread + NORM_EPS)
    offset = shift[...]
    blocks = live[0] // BLOCK

    def fill(b, carry):
        rows = pl.ds(pl.multiple_of(b * BLOCK, BLOCK), BLOCK)
        normed = (conved[rows, :] - average) * factor + offset
        hidden = jnp.maximum(normed, 0.0).astype(BF16)
        own[rows, :] = hidden[:, 0:C]
        table[rows, :] = hidden.astype(F32)
        return carry

    def clear(b, carry):
        rows = pl.ds(pl.multiple_of(b * BLOCK, BLOCK), BLOCK)
        own[rows, :] = jnp.zeros((BLOCK, C), BF16)
        return carry

    lax.fori_loop(0, blocks, fill, 0)
    lax.fori_loop(blocks, V_DEV // BLOCK, clear, 0)
    send_rows_packed(picks, table, stage, out, index, sems)


def conv_kernel(live, maps, own, arrived, weight, middle, out, stats, table, stage, sums, index, sems):
    def fetch(block, slot):
        columns = pl.ds(pl.multiple_of(block * BLOCK, BLOCK), BLOCK)
        return pltpu.make_async_copy(maps.at[:, columns], index.at[slot], sems.at[slot])

    fetch(0, 0).start()
    blocks = live[0] // BLOCK
    lane = lax.broadcasted_iota(jnp.int32, (TAIL, LANES), 1)

    def fill_own(b, carry):
        rows = pl.ds(pl.multiple_of(b * BLOCK, BLOCK), BLOCK)
        table[rows, :] = widen(own[rows, :].astype(F32))
        return carry

    def fill_arrived(p, carry):
        base = pl.multiple_of(V_DEV + p * CAP, CAP)
        rows = arrived[p].astype(F32)
        table[pl.ds(base, C), :] = rows
        tail = None
        for j in range(C // TAIL):
            moved = pltpu.roll(rows[j * TAIL : (j + 1) * TAIL], TAIL * (j + 1), 1)
            tail = moved if tail is None else jnp.where(lane < j * TAIL, tail, moved)
        table[pl.ds(base + C, TAIL), :] = tail
        return carry

    lax.fori_loop(0, V_DEV // BLOCK, fill_own, 0, unroll=2)
    lax.fori_loop(0, DEVICES, fill_arrived, 0, unroll=8)
    table[MISSING : MISSING + 8, :] = jnp.zeros((8, LANES), F32)

    def multiply(slot, p):
        return jnp.dot(stage[slot, p].astype(BF16), weight[p], preferred_element_type=F32)

    def collect(slot, p):
        for c in range(BLOCK):
            low, high = index[slot, p, c], index[slot, MID + 1 + p, c]
            stage[slot, p, c : c + 1, 0:LANES] = table[pl.ds(low, 1), :]
            stage[slot, p, c : c + 1, LANES : 2 * LANES] = table[pl.ds(high, 1), :]

    def center(block):
        rows = pl.ds(pl.multiple_of(block * BLOCK, BLOCK), BLOCK)
        return jnp.dot(table[rows, :].astype(BF16), middle[...], preferred_element_type=F32)

    def finish(block, total):
        out[pl.ds(pl.multiple_of(block * BLOCK, BLOCK), BLOCK), :] = total
        return jnp.sum(total.reshape(BLOCK // 8, 8, LANES), axis=0)

    def step(block, slot):
        fetch(block, slot).wait()

        @pl.when(block + 1 < blocks)
        def _():
            fetch(block + 1, 1 - slot).start()

        before = jnp.maximum(block - 1, 0)
        total = center(before)
        for p in range(PAIRS):
            total = total + multiply(1 - slot, p)
            collect(slot, p)
        part = finish(before, total)
        sums[...] = jnp.where(block > 0, sums[...] + part, 0.0)

    def advance(block, carry):
        for slot in range(2):
            pl.when(block % 2 == slot)(functools.partial(step, block, slot))
        return carry

    sums[...] = jnp.zeros((8, LANES), F32)
    lax.fori_loop(0, blocks, advance, 0)
    last = blocks - 1
    total = center(last)
    for p in range(PAIRS):
        total = total + multiply(last % 2, p)
    sums[...] += finish(last, total)

    count = (blocks * BLOCK).astype(F32)
    average = jnp.sum(sums[...], axis=0, keepdims=True) / count

    def deviate(block, squares):
        rows = pl.ds(pl.multiple_of(block * BLOCK, BLOCK), BLOCK)
        apart = out[rows, :] - average
        return squares + jnp.sum((apart * apart).reshape(BLOCK // 8, 8, LANES), axis=0)

    squares = lax.fori_loop(0, blocks, deviate, jnp.zeros((8, LANES), F32))
    spare = lax.broadcasted_iota(jnp.int32, (1, LANES), 1) >= C
    squares = jnp.where(spare, count, jnp.sum(squares, axis=0, keepdims=True))
    both = jnp.concatenate([average, squares], axis=0)
    stats[...] = jnp.broadcast_to(both[None], (DEVICES, 2, LANES))


def last_kernel(live, conved, stats, gain, shift, out):
    step = pl.program_id(0)
    average, spread = moments(stats)
    factor = gain[...] * lax.rsqrt(spread + NORM_EPS)
    size = conved.shape[0]
    row = lax.broadcasted_iota(jnp.int32, (size, LANES), 0) + step * size
    normed = jnp.maximum((conved[...] - average) * factor + shift[...], 0.0)
    normed = jnp.where(row < live[0], normed, 0.0)
    out[...] = jnp.transpose(normed)[0:C, :].astype(BF16)


def params():
    return pltpu.CompilerParams(vmem_limit_bytes=VMEM_LIMIT)


def send_scratch():
    return [
        pltpu.VMEM((V_DEV, LANES), F32),
        pltpu.VMEM((GROUP, CAP, LANES), F32),
        pltpu.SMEM((SLOTS, GROUP, CAP), jnp.int32),
        pltpu.SemaphoreType.DMA((SLOTS,)),
    ]


def first_send(picks, own):
    return pl.pallas_call(
        first_send_kernel,
        in_specs=[IN_ANY, IN_VMEM],
        out_specs=IN_VMEM,
        out_shape=jax.ShapeDtypeStruct((DEVICES, C, LANES), BF16),
        scratch_shapes=send_scratch(),
        compiler_params=params(),
        name="first_send",
    )(picks, own)


def next_send(picks, live, conved, stats, gain, shift):
    return pl.pallas_call(
        next_send_kernel,
        in_specs=[IN_ANY, IN_SMEM] + [IN_VMEM] * 4,
        out_specs=[IN_VMEM, IN_VMEM],
        out_shape=[
            jax.ShapeDtypeStruct((DEVICES, C, LANES), BF16),
            jax.ShapeDtypeStruct((V_DEV, C), BF16),
        ],
        scratch_shapes=send_scratch(),
        compiler_params=params(),
        name="next_send",
    )(picks, live, conved, stats, gain, shift)


@jax.jit
def convolve(live, maps, own, arrived, weight, middle):
    return pl.pallas_call(
        conv_kernel,
        in_specs=[IN_SMEM, IN_ANY] + [IN_VMEM] * 4,
        out_specs=[IN_VMEM, IN_VMEM],
        out_shape=[
            jax.ShapeDtypeStruct((V_DEV, LANES), F32),
            jax.ShapeDtypeStruct((DEVICES, 2, LANES), F32),
        ],
        scratch_shapes=[
            pltpu.VMEM((MISSING + 8, LANES), F32),
            pltpu.VMEM((2, PAIRS, BLOCK, 2 * LANES), F32),
            pltpu.VMEM((8, LANES), F32),
            pltpu.SMEM((2, K3, BLOCK), jnp.int32),
            pltpu.SemaphoreType.DMA((2,)),
        ],
        compiler_params=params(),
        name="sparse_conv",
    )(live, maps, own, arrived, weight, middle)


def last_norm(live, conved, stats, gain, shift):
    size = 2048
    whole = lambda *dims: pl.BlockSpec(dims, lambda i: (0,) * len(dims))
    return pl.pallas_call(
        last_kernel,
        grid=(V_DEV // size,),
        in_specs=[
            IN_SMEM,
            pl.BlockSpec((size, LANES), lambda i: (i, 0)),
            whole(DEVICES, 2, LANES),
            whole(1, LANES),
            whole(1, LANES),
        ],
        out_specs=pl.BlockSpec((C, size), lambda i: (0, i)),
        out_shape=jax.ShapeDtypeStruct((C, V_DEV), BF16),
        compiler_params=params(),
        name="last_norm",
    )(live, conved, stats, gain, shift)


def exchange(parcels):
    return lax.all_to_all(parcels, AXES, split_axis=0, concat_axis=0, tiled=True)


def prepare_weight(weight):
    wide = jnp.pad(weight, ((0, 0), (0, LANES - C), (0, LANES - C)))
    return jnp.concatenate([wide[:MID], wide[MID + 1 :]], axis=1), wide[MID]


def body(
    features, neighbors, send_rows, active_rows, weight_one, weight_two, norm_gain, norm_shift
):
    device = lax.axis_index(AXES)
    live = lax.dynamic_slice_in_dim(active_rows, device, 1)
    gain = jnp.pad(norm_gain, ((0, 0), (0, LANES - C)))
    shift = jnp.pad(norm_shift, ((0, 0), (0, LANES - C)))
    picks = send_rows.reshape(DEVICES // GROUP, GROUP, CAP)

    own = jnp.transpose(features)
    arrived = exchange(first_send(picks, own))
    conved, stats = convolve(live, neighbors, own, arrived, *prepare_weight(weight_one))
    stats = exchange(stats)
    parcels, own = next_send(picks, live, conved, stats, gain[0:1], shift[0:1])
    arrived = exchange(parcels)
    conved, stats = convolve(live, neighbors, own, arrived, *prepare_weight(weight_two))
    stats = exchange(stats)
    return last_norm(live, conved, stats, gain[1:2], shift[1:2])


def solution(mesh):
    placed = (
        P(None, AXES),
        P(None, AXES),
        P(AXES, None),
        P(),
        P(),
        P(),
        P(),
        P(),
    )
    return jax.shard_map(
        body, mesh=mesh, in_specs=placed, out_specs=P(None, AXES), check_vma=False
    )
```

```python
import functools

import jax
import jax.numpy as jnp
from jax import lax
from jax.experimental import pallas as pl
from jax.experimental.pallas import tpu as pltpu
from jax.sharding import PartitionSpec as P

AXES = ("region", "sub")
C = 96
K3 = 27
MID = K3 // 2
PAIRS = MID
BLOCK = 128
LANES = 128
V_DEV = 8192
CAP = 128
PART = 32
GROUP = 8
SLOTS = 4
DEVICES = 128
ARRIVED = DEVICES * CAP
MISSING = V_DEV + ARRIVED
NORM_EPS = 1e-05
VMEM_LIMIT = 60 << 20
TAIL = CAP - C

F32 = jnp.float32
BF16 = jnp.bfloat16
IN_VMEM = pl.BlockSpec(memory_space=pltpu.VMEM)
IN_SMEM = pl.BlockSpec(memory_space=pltpu.SMEM)
IN_ANY = pl.BlockSpec(memory_space=pl.ANY)


def widen(rows):
    return jnp.concatenate([rows, jnp.zeros((rows.shape[0], LANES - C), rows.dtype)], axis=1)


def moments(stats):
    means, squares = stats[:, 0, :], stats[:, 1, :]
    counts = squares[:, LANES - 1 : LANES]
    population = jnp.sum(counts, axis=0, keepdims=True)
    average = jnp.sum(means * counts, axis=0, keepdims=True) / population
    apart = means - average
    spread = jnp.sum(squares + counts * apart * apart, axis=0, keepdims=True) / population
    return average, spread


def send_rows_packed(picks, table, stage, out, index, sems):
    lane = lax.broadcasted_iota(jnp.int32, (TAIL, LANES), 1)
    groups = DEVICES // GROUP

    def fetch(g, slot):
        return pltpu.make_async_copy(picks.at[g], index.at[slot], sems.at[slot])

    def pack(d, j):
        last = stage[j, C:CAP, :]
        for t in range(C // TAIL):
            rows = stage[j, t * TAIL : (t + 1) * TAIL, :]
            moved = pltpu.roll(last, C - t * TAIL, 1)
            out[d, t * TAIL : (t + 1) * TAIL, :] = jnp.where(lane < C, rows, moved).astype(BF16)

    def group(g, slot):
        for j in range(GROUP):
            pack(jnp.maximum(g - 1, 0) * GROUP + j, j)
            for c in range(CAP):
                stage[j, c : c + 1, :] = table[pl.ds(index[slot, j, c], 1), :]

    def advance(r, carry):
        for slot in range(SLOTS):
            g = r * SLOTS + slot
            fetch(g, slot).wait()
            group(g, slot)

            @pl.when(g + SLOTS < groups)
            def _():
                fetch(g + SLOTS, slot).start()

        return carry

    lax.fori_loop(0, groups // SLOTS, advance, 0)
    for j in range(GROUP):
        pack(DEVICES - GROUP + j, j)


def start_picks(picks, index, sems):
    for slot in range(SLOTS):
        pltpu.make_async_copy(picks.at[slot], index.at[slot], sems.at[slot]).start()


def first_send_kernel(picks, own, out, table, stage, index, sems):
    start_picks(picks, index, sems)

    def fill(b, carry):
        rows = pl.ds(pl.multiple_of(b * BLOCK, BLOCK), BLOCK)
        table[rows, :] = widen(own[rows, :].astype(F32))
        return carry

    lax.fori_loop(0, V_DEV // BLOCK, fill, 0)
    send_rows_packed(picks, table, stage, out, index, sems)


def next_send_kernel(
    picks, live, conved, stats, gain, shift, out, own, table, stage, index, sems
):
    start_picks(picks, index, sems)
    average, spread = moments(stats)
    factor = gain[...] * lax.rsqrt(spread + NORM_EPS)
    offset = shift[...]
    blocks = live[0] // BLOCK

    def fill(b, carry):
        rows = pl.ds(pl.multiple_of(b * BLOCK, BLOCK), BLOCK)
        normed = (conved[rows, :] - average) * factor + offset
        hidden = jnp.maximum(normed, 0.0).astype(BF16)
        own[rows, :] = hidden[:, 0:C]
        table[rows, :] = hidden.astype(F32)
        return carry

    def clear(b, carry):
        rows = pl.ds(pl.multiple_of(b * BLOCK, BLOCK), BLOCK)
        own[rows, :] = jnp.zeros((BLOCK, C), BF16)
        return carry

    lax.fori_loop(0, blocks, fill, 0)
    lax.fori_loop(blocks, V_DEV // BLOCK, clear, 0)
    send_rows_packed(picks, table, stage, out, index, sems)


def conv_kernel(
    live, maps, own, parcels, weight, middle, out, stats, table, stage, sums, arrived, index, sems, parts
):
    def fetch(block, slot):
        columns = pl.ds(pl.multiple_of(block * BLOCK, BLOCK), BLOCK)
        return pltpu.make_async_copy(maps.at[:, columns], index.at[slot], sems.at[slot])

    def receive(part):
        peers = pl.ds(part * PART, PART)
        return pltpu.make_async_copy(parcels.at[peers], arrived.at[peers], parts.at[part])

    for part in range(DEVICES // PART):
        receive(part).start()
    fetch(0, 0).start()
    blocks = live[0] // BLOCK
    lane = lax.broadcasted_iota(jnp.int32, (TAIL, LANES), 1)

    def fill_own(b, carry):
        rows = pl.ds(pl.multiple_of(b * BLOCK, BLOCK), BLOCK)
        table[rows, :] = widen(own[rows, :].astype(F32))
        return carry

    def fill_arrived(p, carry):
        base = pl.multiple_of(V_DEV + p * CAP, CAP)
        rows = arrived[p].astype(F32)
        table[pl.ds(base, C), :] = rows
        tail = None
        for j in range(C // TAIL):
            moved = pltpu.roll(rows[j * TAIL : (j + 1) * TAIL], TAIL * (j + 1), 1)
            tail = moved if tail is None else jnp.where(lane < j * TAIL, tail, moved)
        table[pl.ds(base + C, TAIL), :] = tail
        return carry

    lax.fori_loop(0, V_DEV // BLOCK, fill_own, 0, unroll=2)
    for part in range(DEVICES // PART):
        receive(part).wait()
        lax.fori_loop(part * PART, (part + 1) * PART, fill_arrived, 0, unroll=8)
    table[MISSING : MISSING + 8, :] = jnp.zeros((8, LANES), F32)

    def multiply(slot, p):
        return jnp.dot(stage[slot, p].astype(BF16), weight[p], preferred_element_type=F32)

    def collect(slot, p):
        for c in range(BLOCK):
            low, high = index[slot, p, c], index[slot, MID + 1 + p, c]
            stage[slot, p, c : c + 1, 0:LANES] = table[pl.ds(low, 1), :]
            stage[slot, p, c : c + 1, LANES : 2 * LANES] = table[pl.ds(high, 1), :]

    def center(block):
        rows = pl.ds(pl.multiple_of(block * BLOCK, BLOCK), BLOCK)
        return jnp.dot(table[rows, :].astype(BF16), middle[...], preferred_element_type=F32)

    def finish(block, total):
        out[pl.ds(pl.multiple_of(block * BLOCK, BLOCK), BLOCK), :] = total
        return jnp.sum(total.reshape(BLOCK // 8, 8, LANES), axis=0)

    def step(block, slot):
        fetch(block, slot).wait()

        @pl.when(block + 1 < blocks)
        def _():
            fetch(block + 1, 1 - slot).start()

        before = jnp.maximum(block - 1, 0)
        total = center(before)
        for p in range(PAIRS):
            total = total + multiply(1 - slot, p)
            collect(slot, p)
        part = finish(before, total)
        sums[...] = jnp.where(block > 0, sums[...] + part, 0.0)

    def advance(block, carry):
        for slot in range(2):
            pl.when(block % 2 == slot)(functools.partial(step, block, slot))
        return carry

    sums[...] = jnp.zeros((8, LANES), F32)
    lax.fori_loop(0, blocks, advance, 0)
    last = blocks - 1
    total = center(last)
    for p in range(PAIRS):
        total = total + multiply(last % 2, p)
    sums[...] += finish(last, total)

    count = (blocks * BLOCK).astype(F32)
    average = jnp.sum(sums[...], axis=0, keepdims=True) / count

    def deviate(block, squares):
        rows = pl.ds(pl.multiple_of(block * BLOCK, BLOCK), BLOCK)
        apart = out[rows, :] - average
        return squares + jnp.sum((apart * apart).reshape(BLOCK // 8, 8, LANES), axis=0)

    squares = lax.fori_loop(0, blocks, deviate, jnp.zeros((8, LANES), F32))
    spare = lax.broadcasted_iota(jnp.int32, (1, LANES), 1) >= C
    squares = jnp.where(spare, count, jnp.sum(squares, axis=0, keepdims=True))
    both = jnp.concatenate([average, squares], axis=0)
    stats[...] = jnp.broadcast_to(both[None], (DEVICES, 2, LANES))


def turn_kernel(conved, out):
    out[...] = jnp.transpose(conved[...])[0:C, :]


def last_kernel(live, turned, stats, gain, shift, out):
    average, spread = moments(stats)
    factor = gain[...] * lax.rsqrt(spread + NORM_EPS)

    def upright(row):
        return jnp.transpose(jnp.broadcast_to(row, (LANES, LANES)))[0:C, 0:1]

    size = turned.shape[1]
    column = lax.broadcasted_iota(jnp.int32, (C, size), 1) + pl.program_id(0) * size
    normed = (turned[...] - upright(average)) * upright(factor) + upright(shift[...])
    out[...] = jnp.where(column < live[0], jnp.maximum(normed, 0.0), 0.0).astype(BF16)


def params():
    return pltpu.CompilerParams(vmem_limit_bytes=VMEM_LIMIT)


def send_scratch():
    return [
        pltpu.VMEM((V_DEV, LANES), F32),
        pltpu.VMEM((GROUP, CAP, LANES), F32),
        pltpu.SMEM((SLOTS, GROUP, CAP), jnp.int32),
        pltpu.SemaphoreType.DMA((SLOTS,)),
    ]


def first_send(picks, own):
    return pl.pallas_call(
        first_send_kernel,
        in_specs=[IN_ANY, IN_VMEM],
        out_specs=IN_VMEM,
        out_shape=jax.ShapeDtypeStruct((DEVICES, C, LANES), BF16),
        scratch_shapes=send_scratch(),
        compiler_params=params(),
        name="first_send",
    )(picks, own)


def next_send(picks, live, conved, stats, gain, shift):
    return pl.pallas_call(
        next_send_kernel,
        in_specs=[IN_ANY, IN_SMEM] + [IN_VMEM] * 4,
        out_specs=[IN_VMEM, IN_VMEM],
        out_shape=[
            jax.ShapeDtypeStruct((DEVICES, C, LANES), BF16),
            jax.ShapeDtypeStruct((V_DEV, C), BF16),
        ],
        scratch_shapes=send_scratch(),
        compiler_params=params(),
        name="next_send",
    )(picks, live, conved, stats, gain, shift)


@jax.jit
def convolve(live, maps, own, arrived, weight, middle):
    return pl.pallas_call(
        conv_kernel,
        in_specs=[IN_SMEM, IN_ANY, IN_VMEM, IN_ANY, IN_VMEM, IN_VMEM],
        out_specs=[IN_VMEM, IN_VMEM],
        out_shape=[
            jax.ShapeDtypeStruct((V_DEV, LANES), F32),
            jax.ShapeDtypeStruct((DEVICES, 2, LANES), F32),
        ],
        scratch_shapes=[
            pltpu.VMEM((MISSING + 8, LANES), F32),
            pltpu.VMEM((2, PAIRS, BLOCK, 2 * LANES), F32),
            pltpu.VMEM((8, LANES), F32),
            pltpu.VMEM((DEVICES, C, LANES), BF16),
            pltpu.SMEM((2, K3, BLOCK), jnp.int32),
            pltpu.SemaphoreType.DMA((2,)),
            pltpu.SemaphoreType.DMA((DEVICES // PART,)),
        ],
        compiler_params=params(),
        name="sparse_conv",
    )(live, maps, own, arrived, weight, middle)


def turn(conved):
    size = 1024
    return pl.pallas_call(
        turn_kernel,
        grid=(V_DEV // size,),
        in_specs=[pl.BlockSpec((size, LANES), lambda i: (i, 0))],
        out_specs=pl.BlockSpec((C, size), lambda i: (0, i)),
        out_shape=jax.ShapeDtypeStruct((C, V_DEV), F32),
        compiler_params=params(),
        cost_estimate=pl.CostEstimate(
            flops=V_DEV * LANES, bytes_accessed=V_DEV * (LANES + C) * 4, transcendentals=0
        ),
        name="turn",
    )(conved)


def last_norm(live, turned, stats, gain, shift):
    size = 4096
    whole = lambda *dims: pl.BlockSpec(dims, lambda i: (0,) * len(dims))
    return pl.pallas_call(
        last_kernel,
        grid=(V_DEV // size,),
        in_specs=[
            IN_SMEM,
            pl.BlockSpec((C, size), lambda i: (0, i)),
            whole(DEVICES, 2, LANES),
            whole(1, LANES),
            whole(1, LANES),
        ],
        out_specs=pl.BlockSpec((C, size), lambda i: (0, i)),
        out_shape=jax.ShapeDtypeStruct((C, V_DEV), BF16),
        compiler_params=params(),
        name="last_norm",
    )(live, turned, stats, gain, shift)


def exchange(parcels):
    return lax.all_to_all(parcels, AXES, split_axis=0, concat_axis=0, tiled=True)


def prepare_weight(weight):
    wide = jnp.pad(weight, ((0, 0), (0, LANES - C), (0, LANES - C)))
    return jnp.concatenate([wide[:MID], wide[MID + 1 :]], axis=1), wide[MID]


def body(
    features, neighbors, send_rows, active_rows, weight_one, weight_two, norm_gain, norm_shift
):
    device = lax.axis_index(AXES)
    live = lax.dynamic_slice_in_dim(active_rows, device, 1)
    gain = jnp.pad(norm_gain, ((0, 0), (0, LANES - C)))
    shift = jnp.pad(norm_shift, ((0, 0), (0, LANES - C)))
    picks = send_rows.reshape(DEVICES // GROUP, GROUP, CAP)

    own = jnp.transpose(features)
    arrived = exchange(first_send(picks, own))
    conved, stats = convolve(live, neighbors, own, arrived, *prepare_weight(weight_one))
    stats = exchange(stats)
    parcels, own = next_send(picks, live, conved, stats, gain[0:1], shift[0:1])
    arrived = exchange(parcels)
    conved, stats = convolve(live, neighbors, own, arrived, *prepare_weight(weight_two))
    stats = exchange(stats)
    return last_norm(live, turn(conved), stats, gain[1:2], shift[1:2])


def solution(mesh):
    placed = (
        P(None, AXES),
        P(None, AXES),
        P(AXES, None),
        P(),
        P(),
        P(),
        P(),
        P(),
    )
    return jax.shard_map(
        body, mesh=mesh, in_specs=placed, out_specs=P(None, AXES), check_vma=False
    )
```

```python
import functools

import jax
import jax.numpy as jnp
from jax import lax
from jax.experimental import pallas as pl
from jax.experimental.pallas import tpu as pltpu
from jax.sharding import PartitionSpec as P

AXES = ("region", "sub")
C = 96
K3 = 27
MID = K3 // 2
PAIRS = MID
BLOCK = 128
LANES = 128
V_DEV = 8192
CAP = 128
PART = 32
GROUP = 8
SLOTS = 4
DEVICES = 128
ARRIVED = DEVICES * CAP
MISSING = V_DEV + ARRIVED
NORM_EPS = 1e-05
VMEM_LIMIT = 60 << 20
TAIL = CAP - C

F32 = jnp.float32
BF16 = jnp.bfloat16
IN_VMEM = pl.BlockSpec(memory_space=pltpu.VMEM)
IN_SMEM = pl.BlockSpec(memory_space=pltpu.SMEM)
IN_ANY = pl.BlockSpec(memory_space=pl.ANY)


def widen(rows):
    return jnp.concatenate([rows, jnp.zeros((rows.shape[0], LANES - C), rows.dtype)], axis=1)


def moments(stats):
    means, squares = stats[:, 0, :], stats[:, 1, :]
    counts = squares[:, LANES - 1 : LANES]
    population = jnp.sum(counts, axis=0, keepdims=True)
    average = jnp.sum(means * counts, axis=0, keepdims=True) / population
    apart = means - average
    spread = jnp.sum(squares + counts * apart * apart, axis=0, keepdims=True) / population
    return average, spread


def send_rows_packed(picks, table, stage, out, index, sems):
    lane = lax.broadcasted_iota(jnp.int32, (TAIL, LANES), 1)
    groups = DEVICES // GROUP

    def fetch(g, slot):
        return pltpu.make_async_copy(picks.at[g], index.at[slot], sems.at[slot])

    def pack(d, j):
        last = stage[j, C:CAP, :]
        for t in range(C // TAIL):
            rows = stage[j, t * TAIL : (t + 1) * TAIL, :]
            moved = pltpu.roll(last, C - t * TAIL, 1)
            out[d, t * TAIL : (t + 1) * TAIL, :] = jnp.where(lane < C, rows, moved).astype(BF16)

    def group(g, slot):
        for j in range(GROUP):
            pack(jnp.maximum(g - 1, 0) * GROUP + j, j)
            for c in range(CAP):
                stage[j, c : c + 1, :] = table[pl.ds(index[slot, j, c], 1), :]

    def advance(r, carry):
        for slot in range(SLOTS):
            g = r * SLOTS + slot
            fetch(g, slot).wait()
            group(g, slot)

            @pl.when(g + SLOTS < groups)
            def _():
                fetch(g + SLOTS, slot).start()

        return carry

    lax.fori_loop(0, groups // SLOTS, advance, 0)
    for j in range(GROUP):
        pack(DEVICES - GROUP + j, j)


def start_picks(picks, index, sems):
    for slot in range(SLOTS):
        pltpu.make_async_copy(picks.at[slot], index.at[slot], sems.at[slot]).start()


def first_send_kernel(picks, own, out, table, stage, index, sems):
    start_picks(picks, index, sems)

    def fill(b, carry):
        rows = pl.ds(pl.multiple_of(b * BLOCK, BLOCK), BLOCK)
        table[rows, :] = widen(own[rows, :].astype(F32))
        return carry

    lax.fori_loop(0, V_DEV // BLOCK, fill, 0, unroll=4)
    send_rows_packed(picks, table, stage, out, index, sems)


def next_send_kernel(
    picks, live, conved, stats, gain, shift, out, own, table, stage, index, sems
):
    start_picks(picks, index, sems)
    average, spread = moments(stats)
    factor = gain[...] * lax.rsqrt(spread + NORM_EPS)
    offset = shift[...]
    blocks = live[0] // BLOCK

    def fill(b, carry):
        rows = pl.ds(pl.multiple_of(b * BLOCK, BLOCK), BLOCK)
        normed = (conved[rows, :] - average) * factor + offset
        hidden = jnp.maximum(normed, 0.0).astype(BF16)
        own[rows, :] = hidden[:, 0:C]
        table[rows, :] = hidden.astype(F32)
        return carry

    def clear(b, carry):
        rows = pl.ds(pl.multiple_of(b * BLOCK, BLOCK), BLOCK)
        own[rows, :] = jnp.zeros((BLOCK, C), BF16)
        return carry

    lax.fori_loop(0, blocks, fill, 0)
    lax.fori_loop(blocks, V_DEV // BLOCK, clear, 0)
    send_rows_packed(picks, table, stage, out, index, sems)


def conv_kernel(
    live, maps, own, parcels, weight, middle, result, stats, table, stage, sums, out, arrived, index, sems, parts, away
):
    def fetch(block, slot):
        columns = pl.ds(pl.multiple_of(block * BLOCK, BLOCK), BLOCK)
        return pltpu.make_async_copy(maps.at[:, columns], index.at[slot], sems.at[slot])

    def receive(part):
        peers = pl.ds(part * PART, PART)
        return pltpu.make_async_copy(parcels.at[peers], arrived.at[peers], parts.at[part])

    for part in range(DEVICES // PART):
        receive(part).start()
    fetch(0, 0).start()
    blocks = live[0] // BLOCK
    lane = lax.broadcasted_iota(jnp.int32, (TAIL, LANES), 1)

    def fill_own(b, carry):
        rows = pl.ds(pl.multiple_of(b * BLOCK, BLOCK), BLOCK)
        table[rows, :] = widen(own[rows, :].astype(F32))
        return carry

    def fill_arrived(p, carry):
        base = pl.multiple_of(V_DEV + p * CAP, CAP)
        rows = arrived[p].astype(F32)
        table[pl.ds(base, C), :] = rows
        tail = None
        for j in range(C // TAIL):
            moved = pltpu.roll(rows[j * TAIL : (j + 1) * TAIL], TAIL * (j + 1), 1)
            tail = moved if tail is None else jnp.where(lane < j * TAIL, tail, moved)
        table[pl.ds(base + C, TAIL), :] = tail
        return carry

    lax.fori_loop(0, V_DEV // BLOCK, fill_own, 0, unroll=2)
    for part in range(DEVICES // PART):
        receive(part).wait()
        lax.fori_loop(part * PART, (part + 1) * PART, fill_arrived, 0, unroll=8)
    table[MISSING : MISSING + 8, :] = jnp.zeros((8, LANES), F32)

    def multiply(slot, p):
        return jnp.dot(stage[slot, p].astype(BF16), weight[p], preferred_element_type=F32)

    def collect(slot, p):
        for c in range(BLOCK):
            low, high = index[slot, p, c], index[slot, MID + 1 + p, c]
            stage[slot, p, c : c + 1, 0:LANES] = table[pl.ds(low, 1), :]
            stage[slot, p, c : c + 1, LANES : 2 * LANES] = table[pl.ds(high, 1), :]

    def center(block):
        rows = pl.ds(pl.multiple_of(block * BLOCK, BLOCK), BLOCK)
        return jnp.dot(table[rows, :].astype(BF16), middle[...], preferred_element_type=F32)

    def finish(block, total):
        out[pl.ds(pl.multiple_of(block * BLOCK, BLOCK), BLOCK), :] = total
        return jnp.sum(total.reshape(BLOCK // 8, 8, LANES), axis=0)

    def step(block, slot):
        fetch(block, slot).wait()

        @pl.when(block + 1 < blocks)
        def _():
            fetch(block + 1, 1 - slot).start()

        before = jnp.maximum(block - 1, 0)
        total = center(before)
        for p in range(PAIRS):
            total = total + multiply(1 - slot, p)
            collect(slot, p)
        part = finish(before, total)
        sums[...] = jnp.where(block > 0, sums[...] + part, 0.0)

    def advance(block, carry):
        for slot in range(2):
            pl.when(block % 2 == slot)(functools.partial(step, block, slot))
        return carry

    sums[...] = jnp.zeros((8, LANES), F32)
    lax.fori_loop(0, blocks, advance, 0)
    last = blocks - 1
    total = center(last)
    for p in range(PAIRS):
        total = total + multiply(last % 2, p)
    sums[...] += finish(last, total)

    leave = pltpu.make_async_copy(out, result, away)
    leave.start()
    count = (blocks * BLOCK).astype(F32)
    average = jnp.sum(sums[...], axis=0, keepdims=True) / count

    def deviate(block, squares):
        rows = pl.ds(pl.multiple_of(block * BLOCK, BLOCK), BLOCK)
        apart = out[rows, :] - average
        return squares + jnp.sum((apart * apart).reshape(BLOCK // 8, 8, LANES), axis=0)

    squares = lax.fori_loop(0, blocks, deviate, jnp.zeros((8, LANES), F32))
    spare = lax.broadcasted_iota(jnp.int32, (1, LANES), 1) >= C
    squares = jnp.where(spare, count, jnp.sum(squares, axis=0, keepdims=True))
    both = jnp.concatenate([average, squares], axis=0)
    stats[...] = jnp.broadcast_to(both[None], (DEVICES, 2, LANES))
    leave.wait()


def turn_kernel(conved, out):
    out[...] = jnp.transpose(conved[...])[0:C, :]


def last_kernel(live, turned, stats, gain, shift, out):
    average, spread = moments(stats)
    factor = gain[...] * lax.rsqrt(spread + NORM_EPS)

    def upright(row):
        return jnp.transpose(jnp.broadcast_to(row, (LANES, LANES)))[0:C, 0:1]

    size = turned.shape[1]
    column = lax.broadcasted_iota(jnp.int32, (C, size), 1) + pl.program_id(0) * size
    normed = (turned[...] - upright(average)) * upright(factor) + upright(shift[...])
    out[...] = jnp.where(column < live[0], jnp.maximum(normed, 0.0), 0.0).astype(BF16)


def params():
    return pltpu.CompilerParams(vmem_limit_bytes=VMEM_LIMIT)


def send_scratch():
    return [
        pltpu.VMEM((V_DEV, LANES), F32),
        pltpu.VMEM((GROUP, CAP, LANES), F32),
        pltpu.SMEM((SLOTS, GROUP, CAP), jnp.int32),
        pltpu.SemaphoreType.DMA((SLOTS,)),
    ]


def first_send(picks, own):
    return pl.pallas_call(
        first_send_kernel,
        in_specs=[IN_ANY, IN_VMEM],
        out_specs=IN_VMEM,
        out_shape=jax.ShapeDtypeStruct((DEVICES, C, LANES), BF16),
        scratch_shapes=send_scratch(),
        compiler_params=params(),
        name="first_send",
    )(picks, own)


def next_send(picks, live, conved, stats, gain, shift):
    return pl.pallas_call(
        next_send_kernel,
        in_specs=[IN_ANY, IN_SMEM] + [IN_VMEM] * 4,
        out_specs=[IN_VMEM, IN_VMEM],
        out_shape=[
            jax.ShapeDtypeStruct((DEVICES, C, LANES), BF16),
            jax.ShapeDtypeStruct((V_DEV, C), BF16),
        ],
        scratch_shapes=send_scratch(),
        compiler_params=params(),
        name="next_send",
    )(picks, live, conved, stats, gain, shift)


@jax.jit
def convolve(live, maps, own, arrived, weight, middle):
    return pl.pallas_call(
        conv_kernel,
        in_specs=[IN_SMEM, IN_ANY, IN_VMEM, IN_ANY, IN_VMEM, IN_VMEM],
        out_specs=[IN_ANY, IN_VMEM],
        out_shape=[
            jax.ShapeDtypeStruct((V_DEV, LANES), F32),
            jax.ShapeDtypeStruct((DEVICES, 2, LANES), F32),
        ],
        scratch_shapes=[
            pltpu.VMEM((MISSING + 8, LANES), F32),
            pltpu.VMEM((2, PAIRS, BLOCK, 2 * LANES), F32),
            pltpu.VMEM((8, LANES), F32),
            pltpu.VMEM((V_DEV, LANES), F32),
            pltpu.VMEM((DEVICES, C, LANES), BF16),
            pltpu.SMEM((2, K3, BLOCK), jnp.int32),
            pltpu.SemaphoreType.DMA((2,)),
            pltpu.SemaphoreType.DMA((DEVICES // PART,)),
            pltpu.SemaphoreType.DMA,
        ],
        compiler_params=params(),
        name="sparse_conv",
    )(live, maps, own, arrived, weight, middle)


def turn(conved):
    size = 1024
    return pl.pallas_call(
        turn_kernel,
        grid=(V_DEV // size,),
        in_specs=[pl.BlockSpec((size, LANES), lambda i: (i, 0))],
        out_specs=pl.BlockSpec((C, size), lambda i: (0, i)),
        out_shape=jax.ShapeDtypeStruct((C, V_DEV), F32),
        compiler_params=params(),
        cost_estimate=pl.CostEstimate(
            flops=V_DEV * LANES, bytes_accessed=V_DEV * (LANES + C) * 4, transcendentals=0
        ),
        name="turn",
    )(conved)


def last_norm(live, turned, stats, gain, shift):
    size = 4096
    whole = lambda *dims: pl.BlockSpec(dims, lambda i: (0,) * len(dims))
    return pl.pallas_call(
        last_kernel,
        grid=(V_DEV // size,),
        in_specs=[
            IN_SMEM,
            pl.BlockSpec((C, size), lambda i: (0, i)),
            whole(DEVICES, 2, LANES),
            whole(1, LANES),
            whole(1, LANES),
        ],
        out_specs=pl.BlockSpec((C, size), lambda i: (0, i)),
        out_shape=jax.ShapeDtypeStruct((C, V_DEV), BF16),
        compiler_params=params(),
        name="last_norm",
    )(live, turned, stats, gain, shift)


def exchange(parcels):
    return lax.all_to_all(parcels, AXES, split_axis=0, concat_axis=0, tiled=True)


def prepare_weight(weight):
    wide = jnp.pad(weight, ((0, 0), (0, LANES - C), (0, LANES - C)))
    return jnp.concatenate([wide[:MID], wide[MID + 1 :]], axis=1), wide[MID]


def body(
    features, neighbors, send_rows, active_rows, weight_one, weight_two, norm_gain, norm_shift
):
    device = lax.axis_index(AXES)
    live = lax.dynamic_slice_in_dim(active_rows, device, 1)
    gain = jnp.pad(norm_gain, ((0, 0), (0, LANES - C)))
    shift = jnp.pad(norm_shift, ((0, 0), (0, LANES - C)))
    picks = send_rows.reshape(DEVICES // GROUP, GROUP, CAP)

    own = jnp.transpose(features)
    arrived = exchange(first_send(picks, own))
    conved, stats = convolve(live, neighbors, own, arrived, *prepare_weight(weight_one))
    stats = exchange(stats)
    parcels, own = next_send(picks, live, conved, stats, gain[0:1], shift[0:1])
    arrived = exchange(parcels)
    conved, stats = convolve(live, neighbors, own, arrived, *prepare_weight(weight_two))
    stats = exchange(stats)
    return last_norm(live, turn(conved), stats, gain[1:2], shift[1:2])


def solution(mesh):
    placed = (
        P(None, AXES),
        P(None, AXES),
        P(AXES, None),
        P(),
        P(),
        P(),
        P(),
        P(),
    )
    return jax.shard_map(
        body, mesh=mesh, in_specs=placed, out_specs=P(None, AXES), check_vma=False
    )
```
